256 devices in a mesh: row: 16 (over y, x_hi, core), col: 16 (over z, x_lo).
Axes of the slice: x: 4 (x_hi: 2, x_lo: 2; x = x_hi * 2 + x_lo), y: 4, z: 8, core: 2. Of those that a mesh axis runs over, the one named last changes fastest.
Arguments:
- iterate: bfloat16 [1, 4608, 18432], P(None, 'row', 'col'), may hold values from -0.03125 to 0.03125
- weights: float32 [1, 4608, 18432], P(None, 'row', 'col'), may hold values from -6 to 6
Outputs:
- update: bfloat16 [1, 4608, 18432], P(None, 'row', 'col')
- new_weights: float32 [1, 4608, 18432], P(None, 'row', 'col')
The draws below stay inside these ranges and needn't reach their ends.
All inputs are finite; a program needn't handle non-finite values.
Results may differ from the reference program's by a relative error of at most 0.0064.
Values may be sent and summed in bfloat16 or wider, within the bound.
A program may use at most 64 MiB of HBM per device.

```python
import math
import jax
import jax.numpy as jnp
from jax import lax

D = 4608
FFN = 18432
LAYERS = 1


def block_scale(stream_key, shape, split, smallest, top_value):
    def one(position, shards_of):
        heights = jax.random.uniform(jax.random.fold_in(jax.random.fold_in(stream_key, 6), position), (shards_of,), jnp.float32, smallest / len(split), top_value / len(split))
        return jnp.repeat(jnp.exp(heights), shape[position] // shards_of).reshape((-1,) + (1,) * (len(shape) - position - 1))

    gain = one(*split[0])
    for cut in split[1:]:
        gain = gain * one(*cut)
    return gain


def bell_draw(stream_key, dims, deviation, bound, pieces=(), kind=jnp.bfloat16):
    level = block_scale(stream_key, dims, pieces, -0.22, 0.18) if pieces else 1.0
    values = jax.random.normal(stream_key, dims, jnp.float32) * deviation * level
    return jnp.minimum(jnp.maximum(values, -bound), bound).astype(kind)


def setup_inputs(seed: int = 0) -> dict:
    key_of = jax.random.split(jax.random.key(seed), 3)
    return {
        "iterate": bell_draw(key_of[0], (LAYERS, D, FFN), (2 * FFN) ** -0.5, 0.03125, ((1, 16), (2, 16))),
        "weights": bell_draw(key_of[1], (LAYERS, D, FFN), 1.0, 6.0, ((1, 16), (2, 16)), jnp.float32),
    }


coef_linear = 3.4445
coef_cubic = -4.775
coef_quintic = 2.0315
step_size = 0.02

def one_layer(matrix, weight_layer):
    gram = lax.dot_general(matrix, matrix, (((1,), (1,)), ((), ())), preferred_element_type=jnp.float32)
    gram_low = gram.astype(jnp.bfloat16)
    square = jnp.dot(gram_low, gram_low, preferred_element_type=jnp.float32)
    poly = (coef_cubic * gram + coef_quintic * square).astype(jnp.bfloat16)
    product = jnp.dot(poly, matrix, preferred_element_type=jnp.float32)
    update = (math.sqrt(FFN) * (coef_linear * matrix.astype(jnp.float32) + product)).astype(jnp.bfloat16)
    new_layer = weight_layer - step_size * update.astype(jnp.float32)
    return (update, new_layer)

def reference(iterate, weights):
    updates = []
    layers_new = []
    for layer in range(LAYERS):
        update, new_layer = one_layer(iterate[layer], weights[layer])
        updates.append(update)
        layers_new.append(new_layer)
    return (jnp.stack(updates), jnp.stack(layers_new))
```

```python
import functools
import math

import jax
import jax.numpy as jnp
from jax import lax
from jax.experimental import pallas as pl
from jax.experimental.pallas import tpu as pltpu
from jax.sharding import PartitionSpec as P

MESH = pl.DeviceIdType.MESH

FFN = 18432
coef_linear = 3.4445
coef_cubic = -4.775
coef_quintic = 2.0315
step_size = 0.02

T = 288
H = 144
N = 1152
S = 72
C = 384
NC = N // C
N_COPIES = 96

SLOT = {(0, 0): 0, (0, 1): 1, (1, 0): 2, (1, 1): 3, (3, 0): 4, (3, 1): 5, (2, 0): 6, (2, 1): 7}


def nt(a, b):
    return lax.dot_general(a, b, (((1,), (1,)), ((), ())), preferred_element_type=jnp.float32)


def kernel(
    x_ref, w_ref, upd_ref, new_ref,
    xb, xp, gp, stage, rs, xs, xr, ga, gs, yo, ys, yr, vb, zo, zs, zr, ssem, rsem,
):
    r, c = lax.axis_index("row"), lax.axis_index("col")
    core, xh, y = lax.rem(r, 2), lax.rem(r // 2, 2), r // 4
    xl, z = lax.rem(c, 2), c // 2

    def at(y_, xh_, core_, z_, xl_):
        return ((y_ * 2 + xh_) * 2 + core_, z_ * 2 + xl_)

    up = at(lax.rem(y + 1, 4), xh, core, z, xl)
    down = at(lax.rem(y + 3, 4), xh, core, z, xl)
    across = at(y, 1 - xh, core, z, xl)
    other = at(y, xh, 1 - core, z, xl)
    right = at(y, xh, core, lax.rem(z + 1, 8), xl)
    left = at(y, xh, core, lax.rem(z + 7, 8), xl)
    beside = at(y, xh, core, z, 1 - xl)

    barrier = pltpu.get_barrier_semaphore()
    everyone = (up, down, across, other, right, left, beside)
    for device in everyone:
        pl.semaphore_signal(barrier, inc=1, device_id=device, device_id_type=MESH)
    xb[0:T, :] = x_ref[0]
    pl.semaphore_wait(barrier, len(everyone))

    copies = []

    def send(src, dst, device):
        i = len(copies)
        copy = pltpu.make_async_remote_copy(
            src_ref=src, dst_ref=dst, send_sem=ssem.at[i], recv_sem=rsem.at[i],
            device_id=device, device_id_type=MESH,
        )
        copy.start()
        copies.append(copy)
        return copy

    def part(buf, slot, lo, rows, cols):
        return buf.at[pl.ds(SLOT[slot] * T + lo, rows), cols]

    everything = pl.ds(0, N)

    def pass_on(buf, cols, src, dst, device, lo=0, rows=T):
        return send(part(buf, src, lo, rows, cols), part(buf, dst, lo, rows, cols), device)

    cols = everything
    x_up = [pass_on(xb, cols, (0, 0), (3, 0), up, p * H, H) for p in (0, 1)]
    x_down = [pass_on(xb, cols, (0, 0), (1, 0), down, p * H, H) for p in (1, 0)]
    x_across = send(xb.at[pl.ds(0, T), :], xp, across)
    x_other = pass_on(xb, cols, (0, 0), (0, 1), other)
    x_up[0].wait_recv()
    far = [pass_on(xb, cols, (3, 0), (2, 0), up, 0, H)]
    x_down[0].wait_recv()
    far += [pass_on(xb, cols, (1, 0), (2, 0), down, H, H)]
    x_down[1].wait_recv()
    swaps = [pass_on(xb, cols, (1, 0), (1, 1), other)]
    x_up[1].wait_recv()
    swaps += [pass_on(xb, cols, (3, 0), (3, 1), other)]
    x_across.wait_recv()
    x_other.wait_recv()

    def gram(l):
        def chunk(n, carry):
            lo = pl.multiple_of(n * C, C)
            b = xb[pl.ds(l * N + lo, C), :]
            for part_, a_ref in ((0, xb), (1, xp)):
                g = nt(a_ref[0:T, :], b)
                for q in range(4):
                    gp[l, part_ * 4 + q, :, pl.ds(lo, C)] = g[q * S : (q + 1) * S]
            return carry

        lax.fori_loop(0, NC, chunk, 0)

    def share(k):
        return lax.rem(z + k + 16, 8)

    hops = {(0, 0): 4, (0, 1): 3, (1, 0): 3, (1, 1): 4}
    sign = (1, -1)
    to = (right, left)
    base = {(0, 0): 0, (0, 1): 4, (1, 0): 7, (1, 1): 10}
    moving = {}

    def rs_first(l):
        for way in (0, 1):
            h = hops[l, way]
            stage[l * 2 + way] = gp[l, share(sign[way] * h)].astype(jnp.bfloat16)
            moving[l, way, 0] = send(stage.at[l * 2 + way], rs.at[base[l, way]], to[way])

    def rs_step(l, t):
        for way in (0, 1):
            h = hops[l, way]
            if t < h:
                moving[l, way, t - 1].wait_recv()
                slot = base[l, way] + t - 1
                total = rs[slot].astype(jnp.float32) + gp[l, share(sign[way] * (h - t))]
                rs[slot] = total.astype(jnp.bfloat16)
                moving[l, way, t] = send(rs.at[slot], rs.at[slot + 1], to[way])

    def rs_last(l):
        total = gp[l, share(0)]
        for way in (0, 1):
            h = hops[l, way]
            moving[l, way, h - 1].wait_recv()
            total += rs[base[l, way] + h - 1].astype(jnp.float32)
        gp[l, share(0)] = total
        xs[l] = total.astype(jnp.bfloat16)
        moving[l] = send(xs.at[l], xr.at[l], beside)

    def ag_first(l):
        moving[l].wait_recv()
        total = gp[l, share(0)] + xr[l].astype(jnp.float32)
        ga[l, share(0)] = total.astype(jnp.bfloat16)
        for way in (0, 1):
            mine = ga.at[l, share(0)]
            moving[l, way, 0] = send(mine, mine, to[way])

    def ag_step(l, t):
        for way in (0, 1):
            h = hops[l, way]
            if t < h:
                moving[l, way, t - 1].wait_recv()
                block = ga.at[l, share(-sign[way] * t)]
                moving[l, way, t] = send(block, block, to[way])

    def ag_last(l):
        for way in (0, 1):
            moving[l, way, hops[l, way] - 1].wait_recv()
        for m in range(4):
            two = [ga[l, 2 * m + k].astype(jnp.float32) for k in (0, 1)]
            gs[l, m * H : (m + 1) * H, :] = jnp.concatenate(two, 0).astype(jnp.bfloat16)

    swaps[0].wait_recv()
    gram(0)
    rs_first(0)
    for copy in far:
        copy.wait_recv()
    swaps += [pass_on(xb, cols, (2, 0), (2, 1), other)]
    rs_step(0, 1)
    swaps[1].wait_recv()
    swaps[2].wait_recv()
    gram(1)
    rs_first(1)
    rs_step(0, 2)
    rs_step(1, 1)
    rs_step(0, 3)
    rs_step(1, 2)
    rs_last(0)
    rs_step(1, 3)
    ag_first(0)
    rs_last(1)
    ag_step(0, 1)
    ag_first(1)
    ag_step(0, 2)
    ag_step(1, 1)
    ag_step(0, 3)
    ag_step(1, 2)
    ag_last(0)
    ag_step(1, 3)
    ag_last(1)

    def product(buf, lo, cols):
        rows = slice(lo, lo + T)
        out = jnp.dot(gs[0, rows, :], buf[0:N, cols], preferred_element_type=jnp.float32)
        return out + jnp.dot(gs[1, rows, :], buf[N : 2 * N, cols], preferred_element_type=jnp.float32)

    flight = {}

    def stage1(n):
        cols = slice(n * C, (n + 1) * C)
        ys[n] = product(xb, T, cols).astype(jnp.bfloat16)
        flight[1, n] = send(ys.at[n], yr.at[n], across)
        yo[:, cols] = product(xb, 0, cols)

    def stage2(n):
        cols, sl = slice(n * C, (n + 1) * C), pl.ds(n * C, C)
        flight[1, n].wait_recv()
        total = yo[:, cols] + yr[n].astype(jnp.float32)
        yo[:, cols] = total
        vb[0:T, cols] = total.astype(jnp.bfloat16)
        flight[2, n] = (
            pass_on(vb, sl, (0, 0), (3, 0), up),
            pass_on(vb, sl, (0, 0), (1, 0), down),
            pass_on(vb, sl, (0, 0), (0, 1), other),
        )

    def stage3(n):
        sl = pl.ds(n * C, C)
        flight[2, n][0].wait_recv()
        a = pass_on(vb, sl, (3, 0), (2, 0), up, 0, H)
        flight[2, n][1].wait_recv()
        b = pass_on(vb, sl, (1, 0), (2, 0), down, H, H)
        flight[3, n] = (
            a, b,
            pass_on(vb, sl, (3, 0), (3, 1), other),
            pass_on(vb, sl, (1, 0), (1, 1), other),
        )

    def stage4(n):
        sl = pl.ds(n * C, C)
        flight[3, n][0].wait_recv()
        flight[3, n][1].wait_recv()
        flight[4, n] = pass_on(vb, sl, (2, 0), (2, 1), other)

    def stage5(n):
        cols = slice(n * C, (n + 1) * C)
        flight[2, n][2].wait_recv()
        flight[3, n][2].wait_recv()
        flight[3, n][3].wait_recv()
        flight[4, n].wait_recv()
        zs[n] = product(vb, T, cols).astype(jnp.bfloat16)
        flight[5, n] = send(zs.at[n], zr.at[n], across)
        zo[:, cols] = product(vb, 0, cols)

    def stage6(n):
        cols = slice(n * C, (n + 1) * C)
        flight[5, n].wait_recv()
        product_ = coef_cubic * yo[:, cols] + coef_quintic * (zo[:, cols] + zr[n].astype(jnp.float32))
        update = math.sqrt(FFN) * (coef_linear * x_ref[0, :, cols].astype(jnp.float32) + product_)
        update = update.astype(jnp.bfloat16)
        upd_ref[0, :, cols] = update
        new_ref[0, :, cols] = w_ref[0, :, cols] - step_size * update.astype(jnp.float32)

    for step, n in (
        (stage1, 0), (stage1, 1), (stage2, 0), (stage1, 2), (stage2, 1), (stage3, 0), (stage2, 2),
        (stage3, 1), (stage4, 0), (stage3, 2), (stage5, 0), (stage4, 1), (stage5, 1), (stage4, 2),
        (stage6, 0), (stage5, 2), (stage6, 1), (stage6, 2),
    ):
        step(n)

    for copy in copies:
        copy.wait_send()


def per_device(iterate, weights):
    vmem = pl.BlockSpec(memory_space=pltpu.VMEM)
    bf, f32 = jnp.bfloat16, jnp.float32
    return pl.pallas_call(
        kernel,
        out_shape=(
            jax.ShapeDtypeStruct(iterate.shape, bf),
            jax.ShapeDtypeStruct(weights.shape, f32),
        ),
        in_specs=[vmem, vmem],
        out_specs=(vmem, vmem),
        scratch_shapes=[
            pltpu.VMEM((8 * T, N), bf),
            pltpu.VMEM((T, N), bf),
            pltpu.VMEM((2, 8, S, N), f32),
            pltpu.VMEM((4, S, N), bf),
            pltpu.VMEM((14, S, N), bf),
            pltpu.VMEM((2, S, N), bf),
            pltpu.VMEM((2, S, N), bf),
            pltpu.VMEM((2, 8, S, N), bf),
            pltpu.VMEM((2, 2 * T, N), bf),
            pltpu.VMEM((T, N), f32),
            pltpu.VMEM((NC, T, C), bf),
            pltpu.VMEM((NC, T, C), bf),
            pltpu.VMEM((8 * T, N), bf),
            pltpu.VMEM((T, N), f32),
            pltpu.VMEM((NC, T, C), bf),
            pltpu.VMEM((NC, T, C), bf),
            pltpu.SemaphoreType.DMA((N_COPIES,)),
            pltpu.SemaphoreType.DMA((N_COPIES,)),
        ],
        compiler_params=pltpu.CompilerParams(
            collective_id=0, has_side_effects=True, vmem_limit_bytes=56 * 2**20
        ),
        cost_estimate=pl.CostEstimate(flops=9_200_000_000, bytes_accessed=4_000_000, transcendentals=0),
    )(iterate, weights)


def solution(mesh):
    spec = P(None, "row", "col")
    return jax.shard_map(
        per_device, mesh=mesh, in_specs=(spec, spec), out_specs=(spec, spec), check_vma=False
    )
```

```python
import functools
import math

import jax
import jax.numpy as jnp
from jax import lax
from jax.experimental import pallas as pl
from jax.experimental.pallas import tpu as pltpu
from jax.sharding import PartitionSpec as P

MESH = pl.DeviceIdType.MESH

FFN = 18432
coef_linear = 3.4445
coef_cubic = -4.775
coef_quintic = 2.0315
step_size = 0.02

T = 288
H = 144
N = 1152
K = 8 * T
S = 72
UNITS = ((0, 0, 512), (1, 0, 768), (1, 768, 768), (1, 1536, 768), (0, 512, 512), (0, 1024, 512), (0, 1536, 768))
CHUNKS = (128, 256, 256, 256, 256)
N_COPIES = 192

SLOT = {(0, 0): 0, (0, 1): 1, (1, 0): 2, (1, 1): 3, (3, 0): 4, (3, 1): 5, (2, 0): 6, (2, 1): 7}

HOPS = (4, 3)

ORDER = (
    ("x_own",), ("x_have", "o"), ("gram", 0), ("rs_first", 0), ("rs_step", 0, 1), ("x_far_up",),
    ("x_far_down",), ("rs_step", 0, 2), ("rs_step", 0, 3), ("x_swap", 3), ("x_swap", 1), ("x_have", "x"),
    ("rs_last", 0), ("x_have", 3), ("x_have", 1), ("gram", 2), ("rs_first", 2), ("ag_first", 0), ("x_swap", 2),
    ("gram", 1), ("rs_first", 1), ("gram", 4), ("gram", 5), ("rs_first", 5), ("rs_step", 2, 1), ("x_have", 2),
    ("gram", 3), ("rs_first", 3), ("ag_step", 0, 1), ("rs_step", 1, 1), ("gram", 6), ("rs_first", 6),
    ("rs_step", 5, 1), ("rs_step", 2, 2), ("rs_step", 3, 1), ("ag_step", 0, 2), ("rs_step", 1, 2),
    ("rs_first", 4), ("rs_step", 2, 3), ("rs_step", 6, 1), ("rs_step", 5, 2), ("rs_step", 1, 3),
    ("rs_step", 3, 2), ("rs_last", 2), ("ag_step", 0, 3), ("rs_step", 5, 3), ("rs_step", 4, 1), ("rs_last", 1),
    ("rs_step", 3, 3), ("rs_step", 6, 2), ("ag_first", 2), ("ag_step", 0, 4), ("assemble", 0), ("rs_last", 5),
    ("ag_first", 1), ("rs_step", 4, 2), ("rs_last", 3), ("rs_step", 6, 3), ("ag_step", 2, 1),
    ("ag_step", 1, 1), ("rs_step", 4, 3), ("ag_first", 3), ("rs_last", 6), ("ag_step", 2, 2),
    ("ag_step", 1, 2), ("ag_first", 5), ("rs_last", 4), ("ag_first", 6), ("ag_step", 3, 1), ("ag_step", 2, 3),
    ("ag_step", 1, 3), ("ag_first", 4), ("ag_step", 5, 1), ("ag_step", 6, 1), ("ag_step", 2, 4),
    ("assemble", 2), ("ag_step", 3, 2), ("ag_step", 1, 4), ("assemble", 1), ("ag_step", 4, 1),
    ("ag_step", 5, 2), ("ag_step", 6, 2), ("ag_step", 3, 3), ("ag_step", 4, 2), ("ag_step", 5, 3),
    ("ag_step", 6, 3), ("ag_step", 3, 4), ("assemble", 3), ("y_partner", 0), ("y_partner", 1),
    ("ag_step", 4, 3), ("y_partner", 2), ("ag_step", 5, 4), ("assemble", 5), ("y_partner", 3),
    ("ag_step", 6, 4), ("assemble", 6), ("y_partner", 4), ("ag_step", 4, 4), ("assemble", 4), ("y_own", 0),
    ("v_own", 0), ("y_own", 1), ("y_own", 2), ("y_own", 3), ("v_own", 1), ("y_own", 4), ("v_up", 0),
    ("v_down", 0), ("v_own", 2), ("v_up", 1), ("v_down", 1), ("v_own", 3), ("v_far", 0), ("z_both", 0),
    ("v_up", 2), ("v_down", 2), ("v_own", 4), ("v_far", 1), ("z_both", 1), ("finish", 0), ("v_down", 3),
    ("v_up", 3), ("v_far", 2), ("z_both", 2), ("v_down", 4), ("v_up", 4), ("finish", 1), ("v_far", 3),
    ("z_both", 3), ("v_far", 4), ("finish", 2), ("z_both", 4), ("finish", 3), ("finish", 4),
)


def nt(a, b):
    return lax.dot_general(a, b, (((1,), (1,)), ((), ())), preferred_element_type=jnp.float32)


def kernel(
    x_ref, out_ref,
    xb, xp, gp, stage, rs, xs, xr, ga, gs, yo, ys, yr, vb, zo, zs, zr, ssem, rsem, own_sem,
):
    r, c = lax.axis_index("row"), lax.axis_index("col")
    core, xh, y = lax.rem(r, 2), lax.rem(r // 2, 2), r // 4
    xl, z = lax.rem(c, 2), c // 2
    turn = 1 - 2 * core

    def at(y_, xh_, core_, z_, xl_):
        return ((y_ * 2 + xh_) * 2 + core_, z_ * 2 + xl_)

    up = at(lax.rem(y + 1, 4), xh, core, z, xl)
    down = at(lax.rem(y + 3, 4), xh, core, z, xl)
    across = at(y, 1 - xh, core, z, xl)
    other = at(y, xh, 1 - core, z, xl)
    ways = (
        at(y, xh, core, lax.rem(z + turn + 8, 8), xl),
        at(y, xh, core, lax.rem(z - turn + 8, 8), xl),
    )
    beside = at(y, xh, core, z, 1 - xl)

    barrier = pltpu.get_barrier_semaphore()
    everyone = (up, down, across, other, *ways, beside)
    for device in everyone:
        pl.semaphore_signal(barrier, inc=1, device_id=device, device_id_type=MESH)
    own = pltpu.make_async_copy(x_ref.at[0], xb.at[pl.ds(0, T), :], own_sem)
    own.start()
    pl.semaphore_wait(barrier, len(everyone))
    own.wait()

    copies = []
    flight = {}

    def send(src, dst, device):
        i = len(copies)
        copy = pltpu.make_async_remote_copy(
            src_ref=src, dst_ref=dst, send_sem=ssem.at[i], recv_sem=rsem.at[i],
            device_id=device, device_id_type=MESH,
        )
        copy.start()
        copies.append(copy)
        return copy

    def arrive(*key):
        flight[key].wait_recv()

    def part(buf, slot, lo, rows, cols):
        return buf.at[pl.ds(SLOT[slot] * T + lo, rows), cols]

    def pass_on(buf, cols, src, dst, device, lo=0, rows=T):
        return send(part(buf, src, lo, rows, cols), part(buf, dst, lo, rows, cols), device)

    every = pl.ds(0, N)

    def x_own():
        for p in (0, 1):
            flight["xu", p] = pass_on(xb, every, (0, 0), (3, 0), up, p * H, H)
            flight["xd", 1 - p] = pass_on(xb, every, (0, 0), (1, 0), down, (1 - p) * H, H)
            if p == 0:
                flight["xo"] = pass_on(xb, every, (0, 0), (0, 1), other)
        flight["xx"] = send(xb.at[pl.ds(0, T), :], xp, across)

    def x_far_up():
        arrive("xu", 0)
        flight["xfu"] = pass_on(xb, every, (3, 0), (2, 0), up, 0, H)

    def x_far_down():
        arrive("xd", 1)
        flight["xfd"] = pass_on(xb, every, (1, 0), (2, 0), down, H, H)

    def x_swap(dy):
        if dy == 1:
            arrive("xd", 0)
        elif dy == 3:
            arrive("xu", 1)
        else:
            flight["xfu"].wait_recv()
            flight["xfd"].wait_recv()
        flight["xs", dy] = pass_on(xb, every, (dy, 0), (dy, 1), other)

    def x_have(what):
        if what == "x":
            flight["xx"].wait_recv()
        elif what == "o":
            flight["xo"].wait_recv()
        else:
            arrive("xs", what)

    def gram(n):
        a, lo, w = UNITS[n]
        g = nt((xb, xp)[a][0:T, :], xb[lo : lo + w, :])
        for q in range(4):
            for m in range(2):
                gp[n][q * 2 + m] = g[q * S : (q + 1) * S, m * (w // 2) : (m + 1) * (w // 2)]

    def share(k):
        return lax.rem(z + turn * k + 16, 8)

    def rs_first(n):
        for way, h in enumerate(HOPS):
            stage[n][way] = gp[n][share((h, -h)[way])].astype(jnp.bfloat16)
            flight["r", n, way, 0] = send(stage[n].at[way], rs[n].at[way * 4], ways[way])

    def rs_step(n, t):
        for way, h in enumerate(HOPS):
            if t < h:
                arrive("r", n, way, t - 1)
                slot, k = way * 4 + t - 1, (h - t, t - h)[way]
                total = rs[n][slot].astype(jnp.float32) + gp[n][share(k)]
                rs[n][slot] = total.astype(jnp.bfloat16)
                flight["r", n, way, t] = send(rs[n].at[slot], rs[n].at[slot + 1], ways[way])

    def rs_last(n):
        total = gp[n][share(0)]
        for way, h in enumerate(HOPS):
            arrive("r", n, way, h - 1)
            total += rs[n][way * 4 + h - 1].astype(jnp.float32)
        gp[n][share(0)] = total
        xs[n][...] = total.astype(jnp.bfloat16)
        flight["x", n] = send(xs[n], xr[n], beside)

    def ag_send(n, way, t):
        block = ga[n].at[share((-t, t)[way])]
        flight["g", n, way, t] = send(block, block, ways[way])

    def ag_first(n):
        arrive("x", n)
        total = gp[n][share(0)] + xr[n][...].astype(jnp.float32)
        ga[n][share(0)] = total.astype(jnp.bfloat16)
        for way in (0, 1):
            ag_send(n, way, 0)

    def ag_step(n, t):
        for way, h in enumerate(HOPS):
            if t <= h:
                arrive("g", n, way, t - 1)
                if t < h:
                    ag_send(n, way, t)

    def assemble(n):
        a, lo, w = UNITS[n]
        for m in range(2):
            rows = [ga[n][q * 2 + m].astype(jnp.float32) for q in range(4)]
            cols = slice(lo + m * (w // 2), lo + (m + 1) * (w // 2))
            gs[a * T : (a + 1) * T, cols] = jnp.concatenate(rows, 0).astype(jnp.bfloat16)

    def cols_of(n):
        lo = sum(CHUNKS[:n])
        return slice(lo, lo + CHUNKS[n]), pl.ds(lo, CHUNKS[n])

    def product(rows, buf, cols):
        return jnp.dot(gs[rows, :], buf[:, cols], preferred_element_type=jnp.float32)

    def y_partner(n):
        cols, sl = cols_of(n)
        ys[:, cols] = product(slice(T, 2 * T), xb, cols).astype(jnp.bfloat16)
        flight["y", n] = send(ys.at[:, sl], yr.at[:, sl], across)

    def y_own(n):
        cols, _ = cols_of(n)
        yo[:, cols] = product(slice(0, T), xb, cols)

    def v_own(n):
        cols, sl = cols_of(n)
        arrive("y", n)
        total = yo[:, cols] + yr[:, cols].astype(jnp.float32)
        yo[:, cols] = total
        vb[0:T, cols] = total.astype(jnp.bfloat16)
        flight["vu", n] = pass_on(vb, sl, (0, 0), (3, 0), up)
        flight["vd", n] = pass_on(vb, sl, (0, 0), (1, 0), down)
        flight["vo", n] = pass_on(vb, sl, (0, 0), (0, 1), other)

    def v_up(n):
        _, sl = cols_of(n)
        arrive("vu", n)
        flight["vfu", n] = pass_on(vb, sl, (3, 0), (2, 0), up, 0, H)
        flight["vs", 3, n] = pass_on(vb, sl, (3, 0), (3, 1), other)

    def v_down(n):
        _, sl = cols_of(n)
        arrive("vd", n)
        flight["vfd", n] = pass_on(vb, sl, (1, 0), (2, 0), down, H, H)
        flight["vs", 1, n] = pass_on(vb, sl, (1, 0), (1, 1), other)

    def v_far(n):
        _, sl = cols_of(n)
        arrive("vfu", n)
        arrive("vfd", n)
        flight["vs", 2, n] = pass_on(vb, sl, (2, 0), (2, 1), other)

    def z_both(n):
        cols, sl = cols_of(n)
        arrive("vo", n)
        for dy in (1, 3, 2):
            arrive("vs", dy, n)
        both = product(slice(0, 2 * T), vb, cols)
        zs[:, cols] = both[T:].astype(jnp.bfloat16)
        flight["z", n] = send(zs.at[:, sl], zr.at[:, sl], across)
        zo[:, cols] = both[:T]

    def finish(n):
        cols, _ = cols_of(n)
        arrive("z", n)
        product_ = coef_cubic * yo[:, cols] + coef_quintic * (zo[:, cols] + zr[:, cols].astype(jnp.float32))
        out_ref[0, :, cols] = math.sqrt(FFN) * (coef_linear * xb[0:T, cols].astype(jnp.float32) + product_)

    steps = (
        x_own, x_far_up, x_far_down, x_swap, x_have, gram, rs_first, rs_step, rs_last,
        ag_first, ag_step, assemble, y_partner, y_own, v_own, v_up, v_down, v_far, z_both, finish,
    )
    steps = {step.__name__: step for step in steps}
    for name, *args in ORDER:
        steps[name](*args)

    for copy in copies:
        copy.wait_send()


def per_device(iterate, weights):
    vmem = pl.BlockSpec(memory_space=pltpu.VMEM)
    bf, f32 = jnp.bfloat16, jnp.float32

    def per_unit(dtype, *shape):
        return [pltpu.VMEM((*shape, w // 2), dtype) for _, _, w in UNITS]

    scaled = pl.pallas_call(
        kernel,
        out_shape=jax.ShapeDtypeStruct(weights.shape, f32),
        in_specs=[pl.BlockSpec(memory_space=pltpu.HBM)],
        out_specs=vmem,
        scratch_shapes=[
            pltpu.VMEM((K, N), bf),
            pltpu.VMEM((T, N), bf),
            per_unit(f32, 8, S),
            per_unit(bf, 2, S),
            per_unit(bf, 7, S),
            per_unit(bf, S),
            per_unit(bf, S),
            per_unit(bf, 8, S),
            pltpu.VMEM((2 * T, K), bf),
            pltpu.VMEM((T, N), f32),
            pltpu.VMEM((T, N), bf),
            pltpu.VMEM((T, N), bf),
            pltpu.VMEM((K, N), bf),
            pltpu.VMEM((T, N), f32),
            pltpu.VMEM((T, N), bf),
            pltpu.VMEM((T, N), bf),
            pltpu.SemaphoreType.DMA((N_COPIES,)),
            pltpu.SemaphoreType.DMA((N_COPIES,)),
            pltpu.SemaphoreType.DMA,
        ],
        compiler_params=pltpu.CompilerParams(
            collective_id=0, has_side_effects=True, vmem_limit_bytes=40 * 2**20
        ),
        cost_estimate=pl.CostEstimate(flops=9_200_000_000, bytes_accessed=4_000_000, transcendentals=0),
    )(iterate)
    update = scaled.astype(bf)
    return update, weights - step_size * update.astype(f32)


def solution(mesh):
    spec = P(None, "row", "col")
    return jax.shard_map(
        per_device, mesh=mesh, in_specs=(spec, spec), out_specs=(spec, spec), check_vma=False
    )
```

```python
import functools
import math

import jax
import jax.numpy as jnp
from jax import lax
from jax.experimental import pallas as pl
from jax.experimental.pallas import tpu as pltpu
from jax.sharding import PartitionSpec as P

MESH = pl.DeviceIdType.MESH

FFN = 18432
coef_linear = 3.4445
coef_cubic = -4.775
coef_quintic = 2.0315
step_size = 0.02

T = 288
H = 144
N = 1152
K = 8 * T
S = 72
PLACE = {
    (0, 0, 0): 0, (0, 0, 1): 144, (0, 1, 0): 288, (0, 1, 1): 432,
    (3, 0, 0): 576, (3, 1, 0): 720, (1, 0, 1): 864, (1, 1, 1): 1008,
    (3, 0, 1): 1152, (3, 1, 1): 1296, (1, 0, 0): 1440, (1, 1, 0): 1584,
    (2, 0, 0): 1728, (2, 1, 0): 1872, (2, 0, 1): 2016, (2, 1, 1): 2160,
}

UNITS = ((0, 0, 512), (0, 512, 512), (0, 1024, 512), (1, 0, 512), (1, 512, 512), (1, 1024, 512), (1, 1536, 512), (1, 2048, 256), (0, 1536, 512), (0, 2048, 256))
CHUNKS = (128, 256, 256, 256, 256)
N_COPIES = 256

HOPS = (4, 3)

(
    X_OWN, X_UP, X_DOWN, X_FAR, X_HAVE, GRAM, RS_FIRST, RS_STEP, RS_LAST, AG_FIRST, AG_STEP, ASSEMBLE,
    Y_PARTNER, Y_OWN, V_OWN, V_UP, V_DOWN, V_FAR, Z_BOTH, FINISH,
) = range(20)
ORDER = (
    (X_OWN,), (X_HAVE, 0), (GRAM, 0), (RS_FIRST, 0), (RS_STEP, 0, 1), (X_UP, 0), (X_DOWN, 1), (RS_STEP, 0, 2),
    (X_HAVE, 2), (GRAM, 1), (RS_FIRST, 1), (RS_STEP, 0, 3), (X_UP, 1), (X_DOWN, 0), (X_HAVE, 1),
    (RS_STEP, 1, 1), (GRAM, 3), (RS_FIRST, 3), (RS_LAST, 0), (GRAM, 4), (RS_FIRST, 4), (X_HAVE, 3), (GRAM, 5),
    (RS_FIRST, 5), (RS_STEP, 1, 2), (GRAM, 2), (X_FAR, 0), (RS_STEP, 3, 1), (RS_FIRST, 2), (X_FAR, 1),
    (RS_STEP, 4, 1), (RS_STEP, 5, 1), (RS_STEP, 1, 3), (X_HAVE, 4), (GRAM, 7), (RS_FIRST, 7), (RS_STEP, 3, 2),
    (GRAM, 6), (RS_FIRST, 6), (RS_STEP, 2, 1), (RS_STEP, 4, 2), (RS_LAST, 1), (GRAM, 8), (RS_STEP, 7, 1),
    (RS_STEP, 5, 2), (RS_STEP, 3, 3), (RS_FIRST, 8), (GRAM, 9), (RS_FIRST, 9), (RS_STEP, 6, 1),
    (RS_STEP, 4, 3), (RS_STEP, 2, 2), (RS_STEP, 5, 3), (AG_FIRST, 0), (RS_STEP, 7, 2), (RS_LAST, 3),
    (RS_STEP, 8, 1), (RS_STEP, 9, 1), (RS_LAST, 4), (RS_STEP, 6, 2), (RS_STEP, 2, 3), (AG_FIRST, 3),
    (RS_LAST, 5), (RS_STEP, 7, 3), (AG_STEP, 0, 1), (AG_FIRST, 4), (RS_STEP, 8, 2), (RS_STEP, 6, 3),
    (RS_STEP, 9, 2), (RS_LAST, 2), (RS_LAST, 7), (AG_STEP, 3, 1), (AG_STEP, 0, 2), (RS_STEP, 8, 3),
    (AG_STEP, 4, 1), (RS_LAST, 6), (AG_FIRST, 7), (AG_FIRST, 5), (RS_STEP, 9, 3), (AG_STEP, 3, 2),
    (RS_LAST, 8), (AG_STEP, 0, 3), (AG_FIRST, 6), (AG_STEP, 4, 2), (AG_STEP, 7, 1), (RS_LAST, 9),
    (AG_STEP, 5, 1), (AG_FIRST, 8), (AG_STEP, 0, 4), (ASSEMBLE, 0), (AG_STEP, 3, 3), (AG_STEP, 6, 1),
    (AG_FIRST, 9), (AG_STEP, 4, 3), (AG_STEP, 7, 2), (AG_STEP, 5, 2), (AG_FIRST, 2), (AG_FIRST, 1),
    (AG_STEP, 3, 4), (AG_STEP, 8, 1), (ASSEMBLE, 3), (AG_STEP, 6, 2), (AG_STEP, 9, 1), (AG_STEP, 4, 4),
    (ASSEMBLE, 4), (AG_STEP, 7, 3), (AG_STEP, 5, 3), (AG_STEP, 2, 1), (AG_STEP, 1, 1), (AG_STEP, 8, 2),
    (AG_STEP, 7, 4), (ASSEMBLE, 7), (AG_STEP, 6, 3), (AG_STEP, 5, 4), (ASSEMBLE, 5), (AG_STEP, 9, 2),
    (AG_STEP, 2, 2), (AG_STEP, 1, 2), (AG_STEP, 6, 4), (ASSEMBLE, 6), (AG_STEP, 8, 3), (Y_PARTNER, 0),
    (Y_PARTNER, 1), (AG_STEP, 9, 3), (AG_STEP, 2, 3), (Y_PARTNER, 2), (AG_STEP, 1, 3), (Y_PARTNER, 3),
    (AG_STEP, 8, 4), (ASSEMBLE, 8), (Y_PARTNER, 4), (AG_STEP, 9, 4), (ASSEMBLE, 9), (AG_STEP, 2, 4),
    (ASSEMBLE, 2), (AG_STEP, 1, 4), (ASSEMBLE, 1), (Y_OWN, 0), (V_OWN, 0), (Y_OWN, 1), (V_OWN, 1), (Y_OWN, 2),
    (Y_OWN, 3), (Y_OWN, 4), (V_UP, 0, 0), (V_UP, 1, 0), (V_DOWN, 1, 0), (V_DOWN, 0, 0), (V_OWN, 2),
    (V_UP, 0, 1), (V_DOWN, 1, 1), (V_UP, 1, 1), (V_DOWN, 0, 1), (V_OWN, 3), (V_FAR, 0, 0), (V_FAR, 1, 0),
    (V_UP, 0, 2), (V_DOWN, 1, 2), (Z_BOTH, 0), (V_DOWN, 0, 2), (V_OWN, 4), (V_UP, 1, 2), (V_FAR, 0, 1),
    (V_FAR, 1, 1), (V_UP, 0, 3), (V_DOWN, 1, 3), (Z_BOTH, 1), (V_DOWN, 0, 3), (V_UP, 1, 3), (FINISH, 0),
    (V_FAR, 0, 2), (V_FAR, 1, 2), (V_UP, 0, 4), (V_DOWN, 1, 4), (Z_BOTH, 2), (V_DOWN, 0, 4), (V_UP, 1, 4),
    (V_FAR, 0, 3), (V_FAR, 1, 3), (FINISH, 1), (V_FAR, 0, 4), (V_FAR, 1, 4), (Z_BOTH, 3), (Z_BOTH, 4),
    (FINISH, 2), (FINISH, 3), (FINISH, 4),
)


def nt(a, b):
    return lax.dot_general(a, b, (((1,), (1,)), ((), ())), preferred_element_type=jnp.float32)


def kernel(
    x_ref, out_ref,
    xb, xp, gp, stage, rs, xs, xr, ga, gs, yo, ys, yr, vb, zo, zs, zr, ssem, rsem, own_sem,
):
    r, c = lax.axis_index("row"), lax.axis_index("col")
    core, xh, y = lax.rem(r, 2), lax.rem(r // 2, 2), r // 4
    xl, z = lax.rem(c, 2), c // 2
    turn = 1 - 2 * core

    def at(y_, xh_, core_, z_, xl_):
        return ((y_ * 2 + xh_) * 2 + core_, z_ * 2 + xl_)

    up = at(lax.rem(y + 1, 4), xh, core, z, xl)
    down = at(lax.rem(y + 3, 4), xh, core, z, xl)
    across = at(y, 1 - xh, core, z, xl)
    other = at(y, xh, 1 - core, z, xl)
    ways = (
        at(y, xh, core, lax.rem(z + turn + 8, 8), xl),
        at(y, xh, core, lax.rem(z - turn + 8, 8), xl),
    )
    beside = at(y, xh, core, z, 1 - xl)

    barrier = pltpu.get_barrier_semaphore()
    everyone = (up, down, across, other, *ways, beside)
    for device in everyone:
        pl.semaphore_signal(barrier, inc=1, device_id=device, device_id_type=MESH)
    own = pltpu.make_async_copy(x_ref.at[0], xb.at[pl.ds(0, T), :], own_sem)
    own.start()
    pl.semaphore_wait(barrier, len(everyone))
    own.wait()

    copies = []
    flight = {}

    def send(src, dst, device):
        i = len(copies)
        copy = pltpu.make_async_remote_copy(
            src_ref=src, dst_ref=dst, send_sem=ssem.at[i], recv_sem=rsem.at[i],
            device_id=device, device_id_type=MESH,
        )
        copy.start()
        copies.append(copy)
        return copy

    def arrive(*key):
        flight[key].wait_recv()

    def half(buf, dy, swapped, p, cols):
        return buf.at[pl.ds(PLACE[dy, swapped, p], H), cols]

    def pass_up(buf, dy, p, cols):
        return send(half(buf, dy, 0, p, cols), half(buf, (dy + 3) % 4, 0, p, cols), up)

    def pass_down(buf, dy, p, cols):
        return send(half(buf, dy, 0, p, cols), half(buf, (dy + 1) % 4, 0, p, cols), down)

    def swap(buf, dy, p, cols):
        return send(half(buf, dy, 0, p, cols), half(buf, dy, 1, p, cols), other)

    every = pl.ds(0, N)

    def x_own():
        flight["xu", 0] = pass_up(xb, 0, 0, every)
        flight["xd", 1] = pass_down(xb, 0, 1, every)
        flight["xo",] = send(xb.at[pl.ds(0, T), :], xb.at[pl.ds(T, T), :], other)
        flight["xu", 1] = pass_up(xb, 0, 1, every)
        flight["xd", 0] = pass_down(xb, 0, 0, every)
        flight["xx",] = send(xb.at[pl.ds(0, T), :], xp, across)

    def x_up(p):
        arrive("xu", p)
        if p == 0:
            flight["xf", 0] = pass_up(xb, 3, 0, every)
        flight["xs", 3, p] = swap(xb, 3, p, every)

    def x_down(p):
        arrive("xd", p)
        if p == 1:
            flight["xf", 1] = pass_down(xb, 1, 1, every)
        flight["xs", 1, p] = swap(xb, 1, p, every)

    def x_far(p):
        arrive("xf", p)
        flight["xs", 2, p] = swap(xb, 2, p, every)

    def x_have(what):
        if what == 0:
            arrive("xo")
        elif what == 1:
            arrive("xx")
        else:
            for dy, p in (((3, 0), (1, 1)), ((3, 1), (1, 0)), ((2, 0), (2, 1)))[what - 2]:
                arrive("xs", dy, p)

    def gram(n):
        a, lo, w = UNITS[n]
        g = nt((xb, xp)[a][0:T, :], xb[lo : lo + w, :])
        for q in range(4):
            for m in range(2):
                gp[n][q * 2 + m] = g[q * S : (q + 1) * S, m * (w // 2) : (m + 1) * (w // 2)]

    def share(k):
        return lax.rem(z + turn * k + 16, 8)

    def rs_first(n):
        for way, h in enumerate(HOPS):
            stage[n][way] = gp[n][share((h, -h)[way])].astype(jnp.bfloat16)
            flight["r", n, way, 0] = send(stage[n].at[way], rs[n].at[way * 4], ways[way])

    def rs_step(n, t):
        for way, h in enumerate(HOPS):
            if t < h:
                arrive("r", n, way, t - 1)
                slot, k = way * 4 + t - 1, (h - t, t - h)[way]
                total = rs[n][slot].astype(jnp.float32) + gp[n][share(k)]
                rs[n][slot] = total.astype(jnp.bfloat16)
                flight["r", n, way, t] = send(rs[n].at[slot], rs[n].at[slot + 1], ways[way])

    def rs_last(n):
        total = gp[n][share(0)]
        for way, h in enumerate(HOPS):
            arrive("r", n, way, h - 1)
            total += rs[n][way * 4 + h - 1].astype(jnp.float32)
        gp[n][share(0)] = total
        xs[n][...] = total.astype(jnp.bfloat16)
        flight["x", n] = send(xs[n], xr[n], beside)

    def ag_send(n, way, t):
        block = ga[n].at[share((-t, t)[way])]
        flight["g", n, way, t] = send(block, block, ways[way])

    def ag_first(n):
        arrive("x", n)
        total = gp[n][share(0)] + xr[n][...].astype(jnp.float32)
        ga[n][share(0)] = total.astype(jnp.bfloat16)
        for way in (0, 1):
            ag_send(n, way, 0)

    def ag_step(n, t):
        for way, h in enumerate(HOPS):
            if t <= h:
                arrive("g", n, way, t - 1)
                if t < h:
                    ag_send(n, way, t)

    def assemble(n):
        a, lo, w = UNITS[n]
        for m in range(2):
            rows = [ga[n][q * 2 + m].astype(jnp.float32) for q in range(4)]
            cols = slice(lo + m * (w // 2), lo + (m + 1) * (w // 2))
            gs[a * T : (a + 1) * T, cols] = jnp.concatenate(rows, 0).astype(jnp.bfloat16)

    def cols_of(n):
        lo = sum(CHUNKS[:n])
        return slice(lo, lo + CHUNKS[n]), pl.ds(lo, CHUNKS[n])

    def product(rows, buf, cols):
        return jnp.dot(gs[rows, :], buf[:, cols], preferred_element_type=jnp.float32)

    def y_partner(n):
        cols, sl = cols_of(n)
        ys[:, cols] = product(slice(T, 2 * T), xb, cols).astype(jnp.bfloat16)
        flight["y", n] = send(ys.at[:, sl], yr.at[:, sl], across)

    def y_own(n):
        cols, _ = cols_of(n)
        yo[:, cols] = product(slice(0, T), xb, cols)

    def v_own(n):
        cols, sl = cols_of(n)
        arrive("y", n)
        total = yo[:, cols] + yr[:, cols].astype(jnp.float32)
        yo[:, cols] = total
        vb[0:T, cols] = total.astype(jnp.bfloat16)
        flight["vu", 0, n] = pass_up(vb, 0, 0, sl)
        flight["vd", 1, n] = pass_down(vb, 0, 1, sl)
        flight["vo", n] = send(vb.at[pl.ds(0, T), sl], vb.at[pl.ds(T, T), sl], other)
        flight["vu", 1, n] = pass_up(vb, 0, 1, sl)
        flight["vd", 0, n] = pass_down(vb, 0, 0, sl)

    def v_up(p, n):
        _, sl = cols_of(n)
        arrive("vu", p, n)
        if p == 0:
            flight["vf", 0, n] = pass_up(vb, 3, 0, sl)
        flight["vs", 3, p, n] = swap(vb, 3, p, sl)

    def v_down(p, n):
        _, sl = cols_of(n)
        arrive("vd", p, n)
        if p == 1:
            flight["vf", 1, n] = pass_down(vb, 1, 1, sl)
        flight["vs", 1, p, n] = swap(vb, 1, p, sl)

    def v_far(p, n):
        _, sl = cols_of(n)
        arrive("vf", p, n)
        flight["vs", 2, p, n] = swap(vb, 2, p, sl)

    def z_both(n):
        cols, sl = cols_of(n)
        arrive("vo", n)
        for dy in (1, 3, 2):
            for p in (0, 1):
                arrive("vs", dy, p, n)
        both = product(slice(0, 2 * T), vb, cols)
        zs[:, cols] = both[T:].astype(jnp.bfloat16)
        flight["z", n] = send(zs.at[:, sl], zr.at[:, sl], across)
        zo[:, cols] = both[:T]

    def finish(n):
        cols, _ = cols_of(n)
        arrive("z", n)
        product_ = coef_cubic * yo[:, cols] + coef_quintic * (zo[:, cols] + zr[:, cols].astype(jnp.float32))
        out_ref[0, :, cols] = math.sqrt(FFN) * (coef_linear * xb[0:T, cols].astype(jnp.float32) + product_)

    steps = (
        x_own, x_up, x_down, x_far, x_have, gram, rs_first, rs_step, rs_last,
        ag_first, ag_step, assemble, y_partner, y_own, v_own, v_up, v_down, v_far, z_both, finish,
    )
    for step, *args in ORDER:
        steps[step](*args)

    for copy in copies:
        copy.wait_send()


def per_device(iterate, weights):
    vmem = pl.BlockSpec(memory_space=pltpu.VMEM)
    bf, f32 = jnp.bfloat16, jnp.float32

    def per_unit(dtype, *shape):
        return [pltpu.VMEM((*shape, w // 2), dtype) for _, _, w in UNITS]

    scaled = pl.pallas_call(
        kernel,
        out_shape=jax.ShapeDtypeStruct(weights.shape, f32),
        in_specs=[pl.BlockSpec(memory_space=pltpu.HBM)],
        out_specs=vmem,
        scratch_shapes=[
            pltpu.VMEM((K, N), bf),
            pltpu.VMEM((T, N), bf),
            per_unit(f32, 8, S),
            per_unit(bf, 2, S),
            per_unit(bf, 7, S),
            per_unit(bf, S),
            per_unit(bf, S),
            per_unit(bf, 8, S),
            pltpu.VMEM((2 * T, K), bf),
            pltpu.VMEM((T, N), f32),
            pltpu.VMEM((T, N), bf),
            pltpu.VMEM((T, N), bf),
            pltpu.VMEM((K, N), bf),
            pltpu.VMEM((T, N), f32),
            pltpu.VMEM((T, N), bf),
            pltpu.VMEM((T, N), bf),
            pltpu.SemaphoreType.DMA((N_COPIES,)),
            pltpu.SemaphoreType.DMA((N_COPIES,)),
            pltpu.SemaphoreType.DMA,
        ],
        compiler_params=pltpu.CompilerParams(
            collective_id=0, has_side_effects=True, vmem_limit_bytes=40 * 2**20
        ),
        cost_estimate=pl.CostEstimate(flops=9_200_000_000, bytes_accessed=4_000_000, transcendentals=0),
    )(iterate)
    update = scaled.astype(bf)
    return update, weights - step_size * update.astype(f32)


def solution(mesh):
    spec = P(None, "row", "col")
    return jax.shard_map(
        per_device, mesh=mesh, in_specs=(spec, spec), out_specs=(spec, spec), check_vma=False
    )
```

```python
import functools
import math

import jax
import jax.numpy as jnp
from jax import lax
from jax.experimental import pallas as pl
from jax.experimental.pallas import tpu as pltpu
from jax.sharding import PartitionSpec as P

MESH = pl.DeviceIdType.MESH

FFN = 18432
coef_linear = 3.4445
coef_cubic = -4.775
coef_quintic = 2.0315
step_size = 0.02

T = 288
H = 144
N = 1152
K = 8 * T
S = 72
PLACE = {
    (0, 0, 0): 0, (0, 0, 1): 144, (0, 1, 0): 288, (0, 1, 1): 432,
    (3, 0, 0): 576, (3, 1, 0): 720, (1, 0, 1): 864, (1, 1, 1): 1008,
    (3, 0, 1): 1152, (3, 1, 1): 1296, (1, 0, 0): 1440, (1, 1, 0): 1584,
    (2, 0, 0): 1728, (2, 1, 0): 1872, (2, 0, 1): 2016, (2, 1, 1): 2160,
}

UNITS = ((0, 0, 512), (0, 512, 512), (0, 1024, 512), (1, 0, 512), (1, 512, 512), (1, 1024, 512), (1, 1536, 512), (1, 2048, 256), (0, 1536, 512), (0, 2048, 256))
CHUNKS = (256, 256, 256, 384)
N_COPIES = 256

HOPS = (4, 3)

(
    X_OWN, X_UP, X_DOWN, X_FAR, X_HAVE, GRAM, RS_FIRST, RS_STEP, RS_LAST, AG_FIRST, AG_STEP, ASSEMBLE,
    Y_PARTNER, Y_OWN, V_OWN, V_UP, V_DOWN, V_FAR, Z_BOTH, FINISH,
) = range(20)
ORDER = (
    (X_OWN,), (X_HAVE, 0), (GRAM, 0), (RS_FIRST, 0), (RS_STEP, 0, 1), (X_UP, 0), (X_DOWN, 1), (RS_STEP, 0, 2),
    (X_HAVE, 2), (GRAM, 1), (RS_FIRST, 1), (RS_STEP, 0, 3), (X_UP, 1), (X_DOWN, 0), (X_HAVE, 1),
    (RS_STEP, 1, 1), (GRAM, 4), (RS_FIRST, 4), (GRAM, 3), (X_HAVE, 3), (RS_FIRST, 3), (GRAM, 5), (RS_FIRST, 5),
    (RS_STEP, 1, 2), (RS_LAST, 0), (GRAM, 2), (X_FAR, 0), (X_FAR, 1), (RS_STEP, 4, 1), (RS_FIRST, 2),
    (RS_STEP, 3, 1), (RS_STEP, 5, 1), (RS_STEP, 1, 3), (X_HAVE, 4), (GRAM, 6), (RS_STEP, 4, 2), (RS_FIRST, 6),
    (RS_STEP, 2, 1), (GRAM, 7), (RS_FIRST, 7), (RS_STEP, 3, 2), (GRAM, 9), (RS_LAST, 1), (AG_FIRST, 0),
    (GRAM, 8), (RS_STEP, 4, 3), (RS_STEP, 5, 2), (RS_STEP, 6, 1), (RS_FIRST, 8), (RS_STEP, 2, 2),
    (RS_STEP, 3, 3), (RS_STEP, 7, 1), (RS_LAST, 4), (RS_FIRST, 9), (AG_STEP, 0, 1), (RS_STEP, 5, 3),
    (RS_STEP, 6, 2), (RS_STEP, 2, 3), (AG_FIRST, 4), (RS_LAST, 3), (RS_STEP, 8, 1), (RS_STEP, 7, 2),
    (RS_STEP, 9, 1), (RS_LAST, 5), (AG_STEP, 0, 2), (RS_STEP, 6, 3), (AG_FIRST, 3), (RS_LAST, 2),
    (AG_STEP, 4, 1), (RS_STEP, 7, 3), (AG_FIRST, 5), (RS_STEP, 8, 2), (RS_STEP, 9, 2), (AG_FIRST, 2),
    (RS_LAST, 6), (AG_STEP, 0, 3), (AG_STEP, 3, 1), (RS_LAST, 7), (AG_STEP, 4, 2), (RS_STEP, 8, 3),
    (AG_STEP, 5, 1), (AG_FIRST, 6), (RS_STEP, 9, 3), (AG_FIRST, 7), (AG_STEP, 0, 4), (ASSEMBLE, 0),
    (AG_STEP, 2, 1), (AG_STEP, 3, 2), (RS_LAST, 8), (AG_STEP, 4, 3), (AG_STEP, 5, 2), (RS_LAST, 9),
    (AG_STEP, 6, 1), (AG_STEP, 7, 1), (AG_FIRST, 8), (AG_STEP, 2, 2), (AG_STEP, 4, 4), (ASSEMBLE, 4),
    (AG_STEP, 3, 3), (AG_FIRST, 9), (AG_FIRST, 1), (AG_STEP, 5, 3), (AG_STEP, 6, 2), (AG_STEP, 7, 2),
    (AG_STEP, 8, 1), (AG_STEP, 3, 4), (ASSEMBLE, 3), (AG_STEP, 2, 3), (AG_STEP, 9, 1), (AG_STEP, 5, 4),
    (ASSEMBLE, 5), (AG_STEP, 1, 1), (AG_STEP, 6, 3), (AG_STEP, 7, 3), (AG_STEP, 2, 4), (ASSEMBLE, 2),
    (AG_STEP, 8, 2), (AG_STEP, 9, 2), (AG_STEP, 1, 2), (AG_STEP, 6, 4), (ASSEMBLE, 6), (AG_STEP, 7, 4),
    (ASSEMBLE, 7), (Y_PARTNER, 0), (Y_PARTNER, 1), (AG_STEP, 8, 3), (AG_STEP, 9, 3), (Y_PARTNER, 2),
    (AG_STEP, 1, 3), (Y_PARTNER, 3), (AG_STEP, 8, 4), (ASSEMBLE, 8), (AG_STEP, 9, 4), (ASSEMBLE, 9),
    (AG_STEP, 1, 4), (ASSEMBLE, 1), (Y_OWN, 0), (V_OWN, 0), (Y_OWN, 1), (Y_OWN, 2), (Y_OWN, 3), (V_OWN, 1),
    (V_UP, 0, 0), (V_DOWN, 1, 0), (V_UP, 1, 0), (V_DOWN, 0, 0), (V_OWN, 2), (V_UP, 0, 1), (V_DOWN, 1, 1),
    (V_UP, 1, 1), (V_DOWN, 0, 1), (V_FAR, 0, 0), (V_FAR, 1, 0), (V_OWN, 3), (V_UP, 0, 2), (V_DOWN, 1, 2),
    (Z_BOTH, 0), (V_DOWN, 0, 2), (V_UP, 1, 2), (V_FAR, 0, 1), (V_FAR, 1, 1), (Z_BOTH, 1), (V_UP, 0, 3),
    (V_DOWN, 1, 3), (V_UP, 1, 3), (V_DOWN, 0, 3), (FINISH, 0), (V_FAR, 0, 2), (V_FAR, 1, 2), (Z_BOTH, 2),
    (V_FAR, 1, 3), (V_FAR, 0, 3), (FINISH, 1), (Z_BOTH, 3), (FINISH, 2), (FINISH, 3),
)


def nt(a, b):
    return lax.dot_general(a, b, (((1,), (1,)), ((), ())), preferred_element_type=jnp.float32)


def kernel(
    x_ref, out_ref,
    xb, xp, gp, stage, rs, xs, xr, ga, gs, yo, ys, yr, vb, zo, zs, zr, ssem, rsem, own_sem,
):
    r, c = lax.axis_index("row"), lax.axis_index("col")
    core, xh, y = lax.rem(r, 2), lax.rem(r // 2, 2), r // 4
    xl, z = lax.rem(c, 2), c // 2
    turn = 1 - 2 * core

    def at(y_, xh_, core_, z_, xl_):
        return ((y_ * 2 + xh_) * 2 + core_, z_ * 2 + xl_)

    up = at(lax.rem(y + 1, 4), xh, core, z, xl)
    down = at(lax.rem(y + 3, 4), xh, core, z, xl)
    across = at(y, 1 - xh, core, z, xl)
    other = at(y, xh, 1 - core, z, xl)
    ways = (
        at(y, xh, core, lax.rem(z + turn + 8, 8), xl),
        at(y, xh, core, lax.rem(z - turn + 8, 8), xl),
    )
    beside = at(y, xh, core, z, 1 - xl)

    barrier = pltpu.get_barrier_semaphore()
    everyone = (up, down, across, other, *ways, beside)
    for device in everyone:
        pl.semaphore_signal(barrier, inc=1, device_id=device, device_id_type=MESH)
    own = pltpu.make_async_copy(x_ref.at[0], xb.at[pl.ds(0, T), :], own_sem)
    own.start()
    pl.semaphore_wait(barrier, len(everyone))
    own.wait()

    copies = []
    flight = {}

    def send(src, dst, device):
        i = len(copies)
        copy = pltpu.make_async_remote_copy(
            src_ref=src, dst_ref=dst, send_sem=ssem.at[i], recv_sem=rsem.at[i],
            device_id=device, device_id_type=MESH,
        )
        copy.start()
        copies.append(copy)
        return copy

    def arrive(*key):
        flight[key].wait_recv()

    def half(buf, dy, swapped, p, cols):
        return buf.at[pl.ds(PLACE[dy, swapped, p], H), cols]

    def pass_up(buf, dy, p, cols):
        return send(half(buf, dy, 0, p, cols), half(buf, (dy + 3) % 4, 0, p, cols), up)

    def pass_down(buf, dy, p, cols):
        return send(half(buf, dy, 0, p, cols), half(buf, (dy + 1) % 4, 0, p, cols), down)

    def swap(buf, dy, p, cols):
        return send(half(buf, dy, 0, p, cols), half(buf, dy, 1, p, cols), other)

    every = pl.ds(0, N)

    def x_own():
        flight["xu", 0] = pass_up(xb, 0, 0, every)
        flight["xd", 1] = pass_down(xb, 0, 1, every)
        flight["xo",] = send(xb.at[pl.ds(0, T), :], xb.at[pl.ds(T, T), :], other)
        flight["xu", 1] = pass_up(xb, 0, 1, every)
        flight["xd", 0] = pass_down(xb, 0, 0, every)
        flight["xx",] = send(xb.at[pl.ds(0, T), :], xp, across)

    def x_up(p):
        arrive("xu", p)
        if p == 0:
            flight["xf", 0] = pass_up(xb, 3, 0, every)
        flight["xs", 3, p] = swap(xb, 3, p, every)

    def x_down(p):
        arrive("xd", p)
        if p == 1:
            flight["xf", 1] = pass_down(xb, 1, 1, every)
        flight["xs", 1, p] = swap(xb, 1, p, every)

    def x_far(p):
        arrive("xf", p)
        flight["xs", 2, p] = swap(xb, 2, p, every)

    def x_have(what):
        if what == 0:
            arrive("xo")
        elif what == 1:
            arrive("xx")
        else:
            for dy, p in (((3, 0), (1, 1)), ((3, 1), (1, 0)), ((2, 0), (2, 1)))[what - 2]:
                arrive("xs", dy, p)

    def gram(n):
        a, lo, w = UNITS[n]
        g = nt((xb, xp)[a][0:T, :], xb[lo : lo + w, :])
        for q in range(4):
            for m in range(2):
                gp[n][q * 2 + m] = g[q * S : (q + 1) * S, m * (w // 2) : (m + 1) * (w // 2)]

    def share(k):
        return lax.rem(z + turn * k + 16, 8)

    def rs_first(n):
        for way, h in enumerate(HOPS):
            stage[n][way] = gp[n][share((h, -h)[way])].astype(jnp.bfloat16)
            flight["r", n, way, 0] = send(stage[n].at[way], rs[n].at[way * 4], ways[way])

    def rs_step(n, t):
        for way, h in enumerate(HOPS):
            if t < h:
                arrive("r", n, way, t - 1)
                slot, k = way * 4 + t - 1, (h - t, t - h)[way]
                total = rs[n][slot].astype(jnp.float32) + gp[n][share(k)]
                rs[n][slot] = total.astype(jnp.bfloat16)
                flight["r", n, way, t] = send(rs[n].at[slot], rs[n].at[slot + 1], ways[way])

    def rs_last(n):
        total = gp[n][share(0)]
        for way, h in enumerate(HOPS):
            arrive("r", n, way, h - 1)
            total += rs[n][way * 4 + h - 1].astype(jnp.float32)
        gp[n][share(0)] = total
        xs[n][...] = total.astype(jnp.bfloat16)
        flight["x", n] = send(xs[n], xr[n], beside)

    def ag_send(n, way, t):
        block = ga[n].at[share((-t, t)[way])]
        flight["g", n, way, t] = send(block, block, ways[way])

    def ag_first(n):
        arrive("x", n)
        total = gp[n][share(0)] + xr[n][...].astype(jnp.float32)
        ga[n][share(0)] = total.astype(jnp.bfloat16)
        for way in (0, 1):
            ag_send(n, way, 0)

    def ag_step(n, t):
        for way, h in enumerate(HOPS):
            if t <= h:
                arrive("g", n, way, t - 1)
                if t < h:
                    ag_send(n, way, t)

    def assemble(n):
        a, lo, w = UNITS[n]
        for m in range(2):
            rows = [ga[n][q * 2 + m].astype(jnp.float32) for q in range(4)]
            cols = slice(lo + m * (w // 2), lo + (m + 1) * (w // 2))
            gs[a * T : (a + 1) * T, cols] = jnp.concatenate(rows, 0).astype(jnp.bfloat16)

    def cols_of(n):
        lo = sum(CHUNKS[:n])
        return slice(lo, lo + CHUNKS[n]), pl.ds(lo, CHUNKS[n])

    def product(rows, buf, cols):
        return jnp.dot(gs[rows, :], buf[:, cols], preferred_element_type=jnp.float32)

    def y_partner(n):
        cols, sl = cols_of(n)
        ys[:, cols] = product(slice(T, 2 * T), xb, cols).astype(jnp.bfloat16)
        flight["y", n] = send(ys.at[:, sl], yr.at[:, sl], across)

    def y_own(n):
        cols, _ = cols_of(n)
        yo[:, cols] = product(slice(0, T), xb, cols)

    def v_own(n):
        cols, sl = cols_of(n)
        arrive("y", n)
        total = yo[:, cols] + yr[:, cols].astype(jnp.float32)
        yo[:, cols] = total
        vb[0:T, cols] = total.astype(jnp.bfloat16)
        flight["vu", 0, n] = pass_up(vb, 0, 0, sl)
        flight["vd", 1, n] = pass_down(vb, 0, 1, sl)
        flight["vo", n] = send(vb.at[pl.ds(0, T), sl], vb.at[pl.ds(T, T), sl], other)
        flight["vu", 1, n] = pass_up(vb, 0, 1, sl)
        flight["vd", 0, n] = pass_down(vb, 0, 0, sl)

    def v_up(p, n):
        _, sl = cols_of(n)
        arrive("vu", p, n)
        if p == 0:
            flight["vf", 0, n] = pass_up(vb, 3, 0, sl)
        flight["vs", 3, p, n] = swap(vb, 3, p, sl)

    def v_down(p, n):
        _, sl = cols_of(n)
        arrive("vd", p, n)
        if p == 1:
            flight["vf", 1, n] = pass_down(vb, 1, 1, sl)
        flight["vs", 1, p, n] = swap(vb, 1, p, sl)

    def v_far(p, n):
        _, sl = cols_of(n)
        arrive("vf", p, n)
        flight["vs", 2, p, n] = swap(vb, 2, p, sl)

    def z_both(n):
        cols, sl = cols_of(n)
        arrive("vo", n)
        for dy in (1, 3, 2):
            for p in (0, 1):
                arrive("vs", dy, p, n)
        both = product(slice(0, 2 * T), vb, cols)
        zs[:, cols] = both[T:].astype(jnp.bfloat16)
        flight["z", n] = send(zs.at[:, sl], zr.at[:, sl], across)
        zo[:, cols] = both[:T]

    def finish(n):
        cols, _ = cols_of(n)
        arrive("z", n)
        product_ = coef_cubic * yo[:, cols] + coef_quintic * (zo[:, cols] + zr[:, cols].astype(jnp.float32))
        out_ref[0, :, cols] = math.sqrt(FFN) * (coef_linear * xb[0:T, cols].astype(jnp.float32) + product_)

    steps = (
        x_own, x_up, x_down, x_far, x_have, gram, rs_first, rs_step, rs_last,
        ag_first, ag_step, assemble, y_partner, y_own, v_own, v_up, v_down, v_far, z_both, finish,
    )
    for step, *args in ORDER:
        steps[step](*args)

    for copy in copies:
        copy.wait_send()


def per_device(iterate, weights):
    vmem = pl.BlockSpec(memory_space=pltpu.VMEM)
    bf, f32 = jnp.bfloat16, jnp.float32

    def per_unit(dtype, *shape):
        return [pltpu.VMEM((*shape, w // 2), dtype) for _, _, w in UNITS]

    scaled = pl.pallas_call(
        kernel,
        out_shape=jax.ShapeDtypeStruct(weights.shape, f32),
        in_specs=[pl.BlockSpec(memory_space=pltpu.HBM)],
        out_specs=vmem,
        scratch_shapes=[
            pltpu.VMEM((K, N), bf),
            pltpu.VMEM((T, N), bf),
            per_unit(f32, 8, S),
            per_unit(bf, 2, S),
            per_unit(bf, 7, S),
            per_unit(bf, S),
            per_unit(bf, S),
            per_unit(bf, 8, S),
            pltpu.VMEM((2 * T, K), bf),
            pltpu.VMEM((T, N), f32),
            pltpu.VMEM((T, N), bf),
            pltpu.VMEM((T, N), bf),
            pltpu.VMEM((K, N), bf),
            pltpu.VMEM((T, N), f32),
            pltpu.VMEM((T, N), bf),
            pltpu.VMEM((T, N), bf),
            pltpu.SemaphoreType.DMA((N_COPIES,)),
            pltpu.SemaphoreType.DMA((N_COPIES,)),
            pltpu.SemaphoreType.DMA,
        ],
        compiler_params=pltpu.CompilerParams(
            collective_id=0, has_side_effects=True, vmem_limit_bytes=40 * 2**20
        ),
        cost_estimate=pl.CostEstimate(flops=9_200_000_000, bytes_accessed=4_000_000, transcendentals=0),
    )(iterate)
    update = scaled.astype(bf)
    return update, weights - step_size * update.astype(f32)


def solution(mesh):
    spec = P(None, "row", "col")
    return jax.shard_map(
        per_device, mesh=mesh, in_specs=(spec, spec), out_specs=(spec, spec), check_vma=False
    )
```
